32 devices in a mesh: tm: 4 (over y, x), slab: 8 (over z, core).
Axes of the slice: x: 2, y: 2, z: 4, core: 2. Of those that a mesh axis runs over, the one named last changes fastest.
Arguments:
- initial: float32 [4, 16, 64, 16, 128], P('tm', None, 'slab'), may hold values from -6 to 6
- source: float32 [4, 64, 16, 128], P('tm', 'slab'), may hold values from -6 to 6
- decay_rate: float32 [64, 16, 128], P('slab'), may hold values from 0.01 to 0.2
- observed: float32 [4, 16, 64, 16, 128], P('tm', None, 'slab'), may hold values from -6 to 6
- release: int32 [4, 16], replicated, may hold values from 0 to 3
- smooth_taps: float32 [31], replicated, may hold values from 0.02 to 0.08
Outputs:
- source_gradient: float32 [4, 64, 2048], P('tm', None, 'slab')
- decay_gradient: float32 [4, 64, 2048], P('tm', None, 'slab')
The draws below stay inside these ranges and needn't reach their ends.
All inputs are finite; a program needn't handle non-finite values.
Results may differ from the reference program's by a relative error of at most 0.0003.
Values sent between devices are 32-bit elements; how exact they have to be, the bound alone decides.
A program may use at most 64 MiB of HBM per device.

```python
import math
import jax
import jax.numpy as jnp
from jax import lax

CHANNELS = 16
STEPS = 4
TAPS = 31
NY = 16
NX = 128
NZ = 64
N_TM = 4


def set_ends(result, key, low, high):
    dims = result.shape
    place = [jax.random.randint(jax.random.fold_in(key, axis), (), 0, dims[axis]) for axis in range(len(dims))]
    result = result.at[tuple(place)].set(low)
    longest = dims.index(max(dims))
    place[longest] = (place[longest] + 1) % dims[longest]
    return result.at[tuple(place)].set(high)


def level_of(own_key, shape, pieces, low, top_value):
    def one(axis_at, blocks):
        draws = jax.random.uniform(jax.random.fold_in(jax.random.fold_in(own_key, 6), axis_at), (blocks,), jnp.float32, low / len(pieces), top_value / len(pieces))
        return jnp.repeat(jnp.exp(draws), shape[axis_at] // blocks).reshape((-1,) + (1,) * (len(shape) - axis_at - 1))

    gain = one(*pieces[0])
    for cut in pieces[1:]:
        gain = gain * one(*cut)
    return gain


def scatter_about(key, dims, width, reach, shards=(), kind=jnp.bfloat16):
    values = jax.random.normal(key, dims, jnp.float32) * width
    if len(shards) > 0:
        values = level_of(key, dims, shards, -0.22, 0.18) * values
    return jnp.clip(values, min=-reach, max=reach).astype(kind)


def setup_inputs(seed: int = 0) -> dict:
    keys = jax.random.split(jax.random.key(seed), 7)
    return {
        "initial": scatter_about(keys[0], (N_TM, CHANNELS, NZ, NY, NX), 1.0, 6.0, ((0, 4), (2, 8)), jnp.float32),
        "source": scatter_about(keys[1], (N_TM, NZ, NY, NX), 1.0, 6.0, ((0, 4), (1, 8)), jnp.float32),
        "decay_rate": jnp.clip(jnp.exp(math.log(0.2) - 2.9957323 * jax.random.uniform(keys[2], (NZ, NY, NX), jnp.float32) ** level_of(keys[2], (NZ, NY, NX), ((0, 8),), -0.2, 0.2)), 0.01, 0.2),
        "observed": scatter_about(keys[3], (N_TM, CHANNELS, NZ, NY, NX), 1.0, 6.0, ((0, 4), (2, 8)), jnp.float32),
        "release": set_ends(jax.random.randint(keys[4], (N_TM, CHANNELS), 0, STEPS), jax.random.fold_in(keys[4], 1), 0, STEPS - 1).astype(jnp.int32),
        "smooth_taps": jnp.clip(jax.random.uniform(keys[5], (TAPS,), jnp.float32, 0.02, 0.08), 0.02, 0.08),
    }


vertical_rate = 0.2
lateral_rate = 0.1


def apply_operator(current, decay_rate):
    padded = jnp.pad(current, ((0, 0), (1, 1), (1, 1), (1, 1)))
    vertical = padded[:, 2:, 1:-1, 1:-1] + padded[:, :-2, 1:-1, 1:-1]
    lateral = padded[:, 1:-1, 2:, 1:-1] + padded[:, 1:-1, :-2, 1:-1]
    lateral = lateral + padded[:, 1:-1, 1:-1, 2:] + padded[:, 1:-1, 1:-1, :-2]
    centre = 1.0 - 2.0 * vertical_rate - 4.0 * lateral_rate - decay_rate
    return current * centre + vertical_rate * vertical + lateral_rate * lateral


def smoothing_matrix(smooth_taps, depth):
    count = smooth_taps.shape[0]
    middle = (count - 1) // 2
    rows = jnp.arange(depth, dtype=jnp.int32)[:, None]
    columns = jnp.arange(depth, dtype=jnp.int32)[None, :]
    offset = columns - rows + middle
    match = (offset[:, :, None] == jnp.arange(count, dtype=jnp.int32)[None, None, :]).astype(smooth_taps.dtype)
    return jnp.sum(match * smooth_taps[None, None, :], axis=-1)


def reference(initial, source, decay_rate, observed, release, smooth_taps):
    depth = observed.shape[2]
    matrix = smoothing_matrix(smooth_taps, depth)
    rolled = jnp.roll(observed, N_TM // 2, axis=0)

    def window(items):
        start_field, release_field, target, release_row = items
        states = [start_field]
        current = start_field
        for step_index in range(STEPS):
            chosen = (release_row == step_index).astype(start_field.dtype)
            current = apply_operator(current, decay_rate) + chosen[:, None, None, None] * release_field[None]
            states.append(current)
        adjoint = states[STEPS] - target
        source_grad = jnp.zeros(release_field.shape, start_field.dtype)
        decay_grad = jnp.zeros(release_field.shape, start_field.dtype)
        for step_index in reversed(range(STEPS)):
            decay_grad = decay_grad - jnp.sum(adjoint * states[step_index], axis=0)
            chosen = (release_row == step_index).astype(start_field.dtype)
            source_grad = source_grad + jnp.sum(chosen[:, None, None, None] * adjoint, axis=0)
            if step_index > 0:
                adjoint = apply_operator(adjoint, decay_rate)
        both = jnp.stack([source_grad.reshape(depth, -1), decay_grad.reshape(depth, -1)])
        smoothed = jnp.einsum("ij,bjk->bik", matrix, both, precision=lax.Precision.HIGHEST)
        return smoothed[0], smoothed[1]

    source_rows, decay_rows = lax.map(window, (initial, source, rolled, release))
    return jnp.roll(source_rows, N_TM // 2, axis=0), jnp.roll(decay_rows, N_TM // 2, axis=0)
```

```python
import functools

import jax
import jax.numpy as jnp
from jax import lax
from jax.experimental import pallas as pl
from jax.experimental.pallas import tpu as pltpu
from jax.sharding import PartitionSpec as P

STEPS = 4
LANES = 128
vertical_rate = 0.2
lateral_rate = 0.1

MESH = pl.DeviceIdType.MESH
WIDE = STEPS
SIDE = STEPS - 1


def operator(v, centre, edges):
    left, right, front, back = edges
    middle = v[1:-1]
    count, ny, nx = middle.shape
    flat = middle.reshape(count * ny, nx)
    west = pltpu.roll(flat, 1, axis=1).reshape(middle.shape)
    east = pltpu.roll(flat, nx - 1, axis=1).reshape(middle.shape)
    south = pltpu.roll(flat, 1, axis=0).reshape(middle.shape)
    north = pltpu.roll(flat, count * ny - 1, axis=0).reshape(middle.shape)
    lateral = west * left + east * right + south * front + north * back
    return middle * centre + vertical_rate * (v[2:] + v[:-2]) + lateral


def inside(v, width, low, high):
    return jnp.concatenate([v[:width] * low, v[width:-width], v[-width:] * high], axis=0)


def kernel(
    groups,
    slabs,
    release_ref,
    taps_ref,
    initial_ref,
    source_ref,
    decay_ref,
    observed_ref,
    source_out,
    decay_out,
    start,
    centre,
    field,
    states,
    final,
    target,
    adjoint,
    total,
    turned,
    columns,
    matrix,
    local_sem,
    side_send,
    side_recv,
    obs_send,
    obs_recv,
    halo_send,
    halo_recv,
    turn_send,
    turn_recv,
):
    tm = lax.axis_index("tm")
    slab = lax.axis_index("slab")
    partner = lax.rem(tm + groups // 2, groups)
    channels, _, ny, nx = start.shape
    local = decay_ref.shape[0]
    depth = matrix.shape[0]
    rows = columns.shape[1]
    width = source_out.shape[2]
    has_low = slab > 0
    has_high = slab < slabs - 1

    def local_copies():
        return (
            pltpu.make_async_copy(initial_ref.at[0], start.at[:, pl.ds(WIDE, local)], local_sem.at[0]),
            pltpu.make_async_copy(source_ref.at[0], field.at[pl.ds(SIDE, local)], local_sem.at[1]),
            pltpu.make_async_copy(decay_ref, centre.at[pl.ds(SIDE, local)], local_sem.at[2]),
        )

    def remote(src, dst, send, recv, to_tm, to_slab):
        return pltpu.make_async_remote_copy(
            src_ref=src,
            dst_ref=dst,
            send_sem=send,
            recv_sem=recv,
            device_id=(to_tm, to_slab),
            device_id_type=MESH,
        )

    def to_high():
        other = slab + 1
        return (
            remote(decay_ref.at[pl.ds(local - SIDE, SIDE)], centre.at[pl.ds(0, SIDE)], side_send.at[0], side_recv.at[0], tm, other),
            remote(source_ref.at[0, pl.ds(local - SIDE, SIDE)], field.at[pl.ds(0, SIDE)], side_send.at[1], side_recv.at[1], tm, other),
            remote(initial_ref.at[0, :, pl.ds(local - WIDE, WIDE)], start.at[:, pl.ds(0, WIDE)], side_send.at[2], side_recv.at[2], tm, other),
        )

    def to_low():
        other = slab - 1
        return (
            remote(decay_ref.at[pl.ds(0, SIDE)], centre.at[pl.ds(SIDE + local, SIDE)], side_send.at[3], side_recv.at[3], tm, other),
            remote(source_ref.at[0, pl.ds(0, SIDE)], field.at[pl.ds(SIDE + local, SIDE)], side_send.at[4], side_recv.at[4], tm, other),
            remote(initial_ref.at[0, :, pl.ds(0, WIDE)], start.at[:, pl.ds(WIDE + local, WIDE)], side_send.at[5], side_recv.at[5], tm, other),
        )

    def observation(c):
        return remote(observed_ref.at[0, c], target.at[c], obs_send.at[c], obs_recv.at[c], partner, slab)

    def halo_high(c):
        return remote(
            adjoint.at[c, pl.ds(local, SIDE)], adjoint.at[c, pl.ds(0, SIDE)], halo_send.at[0, c], halo_recv.at[0, c], tm, slab + 1
        )

    def halo_low(c):
        return remote(
            adjoint.at[c, pl.ds(SIDE, SIDE)], adjoint.at[c, pl.ds(SIDE + local, SIDE)], halo_send.at[1, c], halo_recv.at[1, c], tm, slab - 1
        )

    def turn(other):
        return remote(
            turned.at[:, pl.ds((other * width) // nx, rows)],
            columns.at[:, :, pl.ds(pl.multiple_of(slab * local, local), local)],
            turn_send.at[other],
            turn_recv.at[slab],
            partner,
            other,
        )

    for copy in local_copies():
        copy.start()

    barrier = pltpu.get_barrier_semaphore()

    @pl.loop(0, slabs)
    def _(other):
        pl.semaphore_signal(barrier, inc=1, device_id=(partner, other), device_id_type=MESH)

    @pl.when(has_low)
    def _():
        pl.semaphore_signal(barrier, inc=1, device_id=(tm, slab - 1), device_id_type=MESH)

    @pl.when(has_high)
    def _():
        pl.semaphore_signal(barrier, inc=1, device_id=(tm, slab + 1), device_id_type=MESH)

    pl.semaphore_wait(barrier, slabs + has_low.astype(jnp.int32) + has_high.astype(jnp.int32))

    observation(0).start()

    @pl.when(has_high)
    def _():
        for copy in to_high():
            copy.start()

    @pl.when(has_low)
    def _():
        for copy in to_low():
            copy.start()

    @pl.loop(1, channels)
    def _(c):
        observation(c).start()

    @pl.when(jnp.logical_not(has_low))
    def _():
        centre[pl.ds(0, SIDE)] = jnp.zeros((SIDE, ny, nx), jnp.float32)
        field[pl.ds(0, SIDE)] = jnp.zeros((SIDE, ny, nx), jnp.float32)
        start[:, pl.ds(0, WIDE)] = jnp.zeros((channels, WIDE, ny, nx), jnp.float32)
        adjoint[:, pl.ds(0, SIDE)] = jnp.zeros((channels, SIDE, ny, nx), jnp.float32)

    @pl.when(jnp.logical_not(has_high))
    def _():
        centre[pl.ds(SIDE + local, SIDE)] = jnp.zeros((SIDE, ny, nx), jnp.float32)
        field[pl.ds(SIDE + local, SIDE)] = jnp.zeros((SIDE, ny, nx), jnp.float32)
        start[:, pl.ds(WIDE + local, WIDE)] = jnp.zeros((channels, WIDE, ny, nx), jnp.float32)
        adjoint[:, pl.ds(SIDE + local, SIDE)] = jnp.zeros((channels, SIDE, ny, nx), jnp.float32)

    low = jnp.where(has_low, 1.0, 0.0).astype(jnp.float32)
    high = jnp.where(has_high, 1.0, 0.0).astype(jnp.float32)

    taps = taps_ref.shape[0]
    offset = (
        lax.broadcasted_iota(jnp.int32, (depth, depth), 1)
        - lax.broadcasted_iota(jnp.int32, (depth, depth), 0)
        + (taps - 1) // 2
    )
    matrix[...] = jnp.zeros_like(matrix)
    for tap in range(taps):
        matrix[...] += jnp.where(offset == tap, taps_ref[tap], 0.0)

    total[...] = jnp.zeros_like(total)

    x_at = lax.broadcasted_iota(jnp.int32, (ny, nx), 1)
    y_at = lax.broadcasted_iota(jnp.int32, (ny, nx), 0)
    edges = tuple(
        jnp.where(place, 0.0, lateral_rate).astype(jnp.float32)
        for place in (x_at == 0, x_at == nx - 1, y_at == 0, y_at == ny - 1)
    )

    for copy in local_copies():
        copy.wait()

    @pl.when(has_low)
    def _():
        for copy in to_high():
            copy.wait_recv()

    @pl.when(has_high)
    def _():
        for copy in to_low():
            copy.wait_recv()

    centre[...] = (1.0 - 2.0 * vertical_rate - 4.0 * lateral_rate) - centre[...]

    @pl.loop(0, channels)
    def _(c):
        when = release_ref[tm, c]
        current = start[c]
        for step in range(STEPS):
            halo = SIDE - step
            chosen = jnp.where(when == step, 1.0, 0.0).astype(jnp.float32)
            part = pl.ds(step, local + 2 * halo)
            current = operator(current, centre[part], edges) + chosen * field[part]
            if halo:
                current = inside(current, halo, low, high)
                states[c, step] = current[halo:-halo]
            else:
                final[c] = current

    def backward(c):
        when = release_ref[tm, c]
        current = adjoint[c]
        decay_sum = total[1]
        source_sum = total[0]
        for step in reversed(range(STEPS)):
            own = current[step : step + local]
            chosen = jnp.where(when == step, 1.0, 0.0).astype(jnp.float32)
            source_sum = source_sum + chosen * own
            past = states[c, step - 1] if step else start[c, pl.ds(WIDE, local)]
            decay_sum = decay_sum - own * past
            if step:
                halo = step - 1
                current = operator(current, centre[pl.ds(SIDE - halo, local + 2 * halo)], edges)
                if halo:
                    current = inside(current, halo, low, high)
        total[0] = source_sum
        total[1] = decay_sum

    def await_halo(c):
        @pl.when(has_low)
        def _():
            halo_high(c).wait_recv()

        @pl.when(has_high)
        def _():
            halo_low(c).wait_recv()

    @pl.loop(0, channels)
    def _(c):
        observation(c).wait_recv()
        adjoint[c, pl.ds(SIDE, local)] = final[c] - target[c]

        @pl.when(has_high)
        def _():
            halo_high(c).start()

        @pl.when(has_low)
        def _():
            halo_low(c).start()

        @pl.when(c > 0)
        def _():
            await_halo(c - 1)
            backward(c - 1)

    await_halo(channels - 1)
    backward(channels - 1)

    for kind in range(2):
        turned[kind] = jnp.swapaxes(total[kind], 0, 1)

    @pl.loop(0, slabs)
    def _(step):
        turn(lax.rem(slab + slabs // 2 + step, slabs)).start()

    @pl.when(has_high)
    def _():
        for copy in to_high():
            copy.wait_send()

    @pl.when(has_low)
    def _():
        for copy in to_low():
            copy.wait_send()

    @pl.loop(0, channels)
    def _(c):
        observation(c).wait_send()

        @pl.when(has_high)
        def _():
            halo_high(c).wait_send()

        @pl.when(has_low)
        def _():
            halo_low(c).wait_send()

    @pl.loop(0, slabs)
    def _(other):
        remote(
            turned.at[:, pl.ds(0, rows)],
            columns.at[:, :, pl.ds(pl.multiple_of(other * local, local), local)],
            turn_send.at[other],
            turn_recv.at[other],
            partner,
            other,
        ).wait_recv()

    for kind, out in enumerate((source_out, decay_out)):
        for row in range(rows):
            smooth = jnp.dot(
                matrix[...], columns[kind, row], precision=lax.Precision.HIGHEST, preferred_element_type=jnp.float32
            )
            if width < nx:
                smooth = pltpu.roll(smooth, lax.rem(nx - lax.rem(slab * width, nx), nx), axis=1)[:, :width]
                out[0] = smooth
            else:
                out[0, :, pl.ds(row * nx, nx)] = smooth

    @pl.loop(0, slabs)
    def _(other):
        turn(other).wait_send()


def solution(mesh):
    groups, slabs = mesh.shape["tm"], mesh.shape["slab"]
    placed = (
        P("tm", None, "slab", None, None),
        P("tm", "slab", None, None),
        P("slab", None, None),
        P("tm", None, "slab", None, None),
        P(),
        P(),
    )

    def body(initial, source, decay_rate, observed, release, smooth_taps):
        _, channels, local, ny, nx = initial.shape
        depth = local * slabs
        width = ny * nx // slabs
        rows = max(1, width // nx)
        assert groups % 2 == 0 and local >= WIDE
        assert width % nx == 0 or nx % width == 0
        f32 = jnp.float32
        anywhere = pl.BlockSpec(memory_space=pl.ANY)
        scalars = pl.BlockSpec(memory_space=pltpu.SMEM)
        out = jax.ShapeDtypeStruct((1, depth, width), f32)
        dma = pltpu.SemaphoreType.DMA
        return pl.pallas_call(
            functools.partial(kernel, groups, slabs),
            out_shape=(out, out),
            in_specs=[scalars, scalars] + [anywhere] * 4,
            out_specs=[pl.BlockSpec(memory_space=pltpu.VMEM)] * 2,
            scratch_shapes=[
                pltpu.VMEM((channels, local + 2 * WIDE, ny, nx), f32),
                pltpu.VMEM((local + 2 * SIDE, ny, nx), f32),
                pltpu.VMEM((local + 2 * SIDE, ny, nx), f32),
                pltpu.VMEM((channels, STEPS - 1, local, ny, nx), f32),
                pltpu.VMEM((channels, local, ny, nx), f32),
                pltpu.VMEM((channels, local, ny, nx), f32),
                pltpu.VMEM((channels, local + 2 * SIDE, ny, nx), f32),
                pltpu.VMEM((2, local, ny, nx), f32),
                pltpu.VMEM((2, ny, local, nx), f32),
                pltpu.VMEM((2, rows, depth, nx), f32),
                pltpu.VMEM((depth, depth), f32),
                dma((3,)),
                dma((6,)),
                dma((6,)),
                dma((channels,)),
                dma((channels,)),
                dma((2, channels)),
                dma((2, channels)),
                dma((slabs,)),
                dma((slabs,)),
            ],
            compiler_params=pltpu.CompilerParams(
                collective_id=0, has_side_effects=True, vmem_limit_bytes=40 * 1024 * 1024
            ),
        )(release, smooth_taps, initial, source, decay_rate, observed)

    return jax.shard_map(
        body,
        mesh=mesh,
        in_specs=placed,
        out_specs=(P("tm", None, "slab"), P("tm", None, "slab")),
        check_vma=False,
    )
```

```python
import functools

import jax
import jax.numpy as jnp
from jax import lax
from jax.experimental import pallas as pl
from jax.experimental.pallas import tpu as pltpu
from jax.sharding import PartitionSpec as P

STEPS = 4
LANES = 128
vertical_rate = 0.2
lateral_rate = 0.1

MESH = pl.DeviceIdType.MESH
WIDE = STEPS
GROUP = 2
LAG = 1
SIDE = STEPS - 1


def operator(v, centre, edges):
    left, right, front, back = edges
    middle = v[1:-1]
    count, ny, nx = middle.shape
    flat = middle.reshape(count * ny, nx)
    west = pltpu.roll(flat, 1, axis=1).reshape(middle.shape)
    east = pltpu.roll(flat, nx - 1, axis=1).reshape(middle.shape)
    south = pltpu.roll(flat, 1, axis=0).reshape(middle.shape)
    north = pltpu.roll(flat, count * ny - 1, axis=0).reshape(middle.shape)
    lateral = west * left + east * right + south * front + north * back
    return middle * centre + vertical_rate * (v[2:] + v[:-2]) + lateral


def inside(v, width, low, high):
    return jnp.concatenate([v[:width] * low, v[width:-width], v[-width:] * high], axis=0)


def kernel(
    groups,
    slabs,
    release_in,
    taps_in,
    initial_ref,
    source_ref,
    decay_ref,
    observed_ref,
    columns,
    matrix,
    start,
    centre,
    field,
    states,
    target,
    adjoint,
    total,
    turned,
    release_ref,
    taps_ref,
    local_sem,
    side_send,
    side_recv,
    start_send,
    start_recv,
    obs_send,
    obs_recv,
    halo_send,
    halo_recv,
    turn_send,
    turn_recv,
):
    tm = lax.axis_index("tm")
    slab = lax.axis_index("slab")
    partner = lax.rem(tm + groups // 2, groups)
    channels, _, ny, nx = start.shape
    local = decay_ref.shape[0]
    parcels = channels // GROUP
    depth = matrix.shape[0]
    rows = columns.shape[1]
    width = ny * nx // slabs
    has_low = slab > 0
    has_high = slab < slabs - 1

    def local_copies():
        return (
            pltpu.make_async_copy(initial_ref.at[0], start.at[:, pl.ds(WIDE, local)], local_sem.at[0]),
            pltpu.make_async_copy(source_ref.at[0], field.at[pl.ds(SIDE, local)], local_sem.at[1]),
            pltpu.make_async_copy(decay_ref, centre.at[pl.ds(SIDE, local)], local_sem.at[2]),
            pltpu.make_async_copy(release_in, release_ref, local_sem.at[3]),
            pltpu.make_async_copy(taps_in, taps_ref, local_sem.at[4]),
        )

    def remote(src, dst, send, recv, to_tm, to_slab):
        return pltpu.make_async_remote_copy(
            src_ref=src,
            dst_ref=dst,
            send_sem=send,
            recv_sem=recv,
            device_id=(to_tm, to_slab),
            device_id_type=MESH,
        )

    def to_high():
        other = slab + 1
        return (
            remote(decay_ref.at[pl.ds(local - SIDE, SIDE)], centre.at[pl.ds(0, SIDE)], side_send.at[0], side_recv.at[0], tm, other),
            remote(source_ref.at[0, pl.ds(local - SIDE, SIDE)], field.at[pl.ds(0, SIDE)], side_send.at[1], side_recv.at[1], tm, other),
        )

    def to_low():
        other = slab - 1
        return (
            remote(decay_ref.at[pl.ds(0, SIDE)], centre.at[pl.ds(SIDE + local, SIDE)], side_send.at[2], side_recv.at[2], tm, other),
            remote(source_ref.at[0, pl.ds(0, SIDE)], field.at[pl.ds(SIDE + local, SIDE)], side_send.at[3], side_recv.at[3], tm, other),
        )

    def span(g):
        return pl.ds(g * GROUP, GROUP)

    def start_high(g):
        return remote(
            initial_ref.at[0, span(g), pl.ds(local - WIDE, WIDE)], start.at[span(g), pl.ds(0, WIDE)], start_send.at[0, g], start_recv.at[0, g], tm, slab + 1
        )

    def start_low(g):
        return remote(
            initial_ref.at[0, span(g), pl.ds(0, WIDE)], start.at[span(g), pl.ds(WIDE + local, WIDE)], start_send.at[1, g], start_recv.at[1, g], tm, slab - 1
        )

    def observation(g):
        return remote(observed_ref.at[0, span(g)], target.at[span(g)], obs_send.at[g], obs_recv.at[g], partner, slab)

    def halo_high(g):
        return remote(
            adjoint.at[span(g), pl.ds(local, SIDE)], adjoint.at[span(g), pl.ds(0, SIDE)], halo_send.at[0, g], halo_recv.at[0, g], tm, slab + 1
        )

    def halo_low(g):
        return remote(
            adjoint.at[span(g), pl.ds(SIDE, SIDE)], adjoint.at[span(g), pl.ds(SIDE + local, SIDE)], halo_send.at[1, g], halo_recv.at[1, g], tm, slab - 1
        )

    def turn(other):
        return remote(
            turned.at[:, pl.ds((other * width) // nx, rows)],
            columns.at[:, :, pl.ds(pl.multiple_of(slab * local, local), local)],
            turn_send.at[other],
            turn_recv.at[slab],
            partner,
            other,
        )

    for copy in local_copies():
        copy.start()

    barrier = pltpu.get_barrier_semaphore()

    @pl.loop(0, slabs)
    def _(other):
        pl.semaphore_signal(barrier, inc=1, device_id=(partner, other), device_id_type=MESH)

    @pl.when(has_low)
    def _():
        pl.semaphore_signal(barrier, inc=1, device_id=(tm, slab - 1), device_id_type=MESH)

    @pl.when(has_high)
    def _():
        pl.semaphore_signal(barrier, inc=1, device_id=(tm, slab + 1), device_id_type=MESH)

    pl.semaphore_wait(barrier, slabs + has_low.astype(jnp.int32) + has_high.astype(jnp.int32))

    observation(0).start()

    @pl.when(has_high)
    def _():
        for copy in to_high():
            copy.start()

    @pl.when(has_low)
    def _():
        for copy in to_low():
            copy.start()

    @pl.loop(0, parcels)
    def _(g):
        @pl.when(has_high)
        def _():
            start_high(g).start()

        @pl.when(has_low)
        def _():
            start_low(g).start()

        @pl.when(g > 0)
        def _():
            observation(g).start()

    @pl.when(jnp.logical_not(has_low))
    def _():
        centre[pl.ds(0, SIDE)] = jnp.zeros((SIDE, ny, nx), jnp.float32)
        field[pl.ds(0, SIDE)] = jnp.zeros((SIDE, ny, nx), jnp.float32)
        start[:, pl.ds(0, WIDE)] = jnp.zeros((channels, WIDE, ny, nx), jnp.float32)
        adjoint[:, pl.ds(0, SIDE)] = jnp.zeros((channels, SIDE, ny, nx), jnp.float32)

    @pl.when(jnp.logical_not(has_high))
    def _():
        centre[pl.ds(SIDE + local, SIDE)] = jnp.zeros((SIDE, ny, nx), jnp.float32)
        field[pl.ds(SIDE + local, SIDE)] = jnp.zeros((SIDE, ny, nx), jnp.float32)
        start[:, pl.ds(WIDE + local, WIDE)] = jnp.zeros((channels, WIDE, ny, nx), jnp.float32)
        adjoint[:, pl.ds(SIDE + local, SIDE)] = jnp.zeros((channels, SIDE, ny, nx), jnp.float32)

    low = jnp.where(has_low, 1.0, 0.0).astype(jnp.float32)
    high = jnp.where(has_high, 1.0, 0.0).astype(jnp.float32)

    for copy in local_copies():
        copy.wait()

    taps = taps_ref.shape[0]
    offset = (
        lax.broadcasted_iota(jnp.int32, (depth, depth), 1)
        - lax.broadcasted_iota(jnp.int32, (depth, depth), 0)
        + (taps - 1) // 2
    )
    matrix[...] = jnp.zeros_like(matrix)
    for tap in range(taps):
        matrix[...] += jnp.where(offset == tap, taps_ref[tap], 0.0)

    total[...] = jnp.zeros_like(total)

    x_at = lax.broadcasted_iota(jnp.int32, (ny, nx), 1)
    y_at = lax.broadcasted_iota(jnp.int32, (ny, nx), 0)
    edges = tuple(
        jnp.where(place, 0.0, lateral_rate).astype(jnp.float32)
        for place in (x_at == 0, x_at == nx - 1, y_at == 0, y_at == ny - 1)
    )

    @pl.when(has_low)
    def _():
        for copy in to_high():
            copy.wait_recv()

    @pl.when(has_high)
    def _():
        for copy in to_low():
            copy.wait_recv()

    centre[...] = (1.0 - 2.0 * vertical_rate - 4.0 * lateral_rate) - centre[...]

    def forward(c):
        when = release_ref[tm, c]
        current = start[c]
        for step in range(STEPS):
            halo = SIDE - step
            chosen = jnp.where(when == step, 1.0, 0.0).astype(jnp.float32)
            part = pl.ds(step, local + 2 * halo)
            current = operator(current, centre[part], edges) + chosen * field[part]
            if halo:
                current = inside(current, halo, low, high)
                states[c, step] = current[halo:-halo]
            else:
                adjoint[c, pl.ds(SIDE, local)] = current

    def backward(c):
        when = release_ref[tm, c]
        current = adjoint[c]
        decay_sum = total[1]
        source_sum = total[0]
        for step in reversed(range(STEPS)):
            own = current[step : step + local]
            chosen = jnp.where(when == step, 1.0, 0.0).astype(jnp.float32)
            source_sum = source_sum + chosen * own
            past = states[c, step - 1] if step else start[c, pl.ds(WIDE, local)]
            decay_sum = decay_sum - own * past
            if step:
                halo = step - 1
                current = operator(current, centre[pl.ds(SIDE - halo, local + 2 * halo)], edges)
                if halo:
                    current = inside(current, halo, low, high)
        total[0] = source_sum
        total[1] = decay_sum

    def members(g, action):
        for c in range(GROUP):
            action(g * GROUP + c)

    def settle(g):
        @pl.when(has_low)
        def _():
            halo_high(g).wait_recv()

        @pl.when(has_high)
        def _():
            halo_low(g).wait_recv()

        members(g, backward)

    @pl.loop(0, parcels)
    def _(g):
        @pl.when(has_low)
        def _():
            start_high(g).wait_recv()

        @pl.when(has_high)
        def _():
            start_low(g).wait_recv()

        members(g, forward)
        observation(g).wait_recv()
        adjoint[span(g), pl.ds(SIDE, local)] = adjoint[span(g), pl.ds(SIDE, local)] - target[span(g)]

        @pl.when(has_high)
        def _():
            halo_high(g).start()

        @pl.when(has_low)
        def _():
            halo_low(g).start()

        @pl.when(g >= LAG)
        def _():
            settle(g - LAG)

    @pl.loop(parcels - LAG, parcels)
    def _(g):
        settle(g)

    for kind in range(2):
        turned[kind] = jnp.swapaxes(total[kind], 0, 1)

    @pl.loop(0, slabs)
    def _(step):
        turn(lax.rem(slab + slabs // 2 + step, slabs)).start()

    @pl.when(has_high)
    def _():
        for copy in to_high():
            copy.wait_send()

    @pl.when(has_low)
    def _():
        for copy in to_low():
            copy.wait_send()

    @pl.loop(0, parcels)
    def _(g):
        observation(g).wait_send()

        @pl.when(has_high)
        def _():
            halo_high(g).wait_send()
            start_high(g).wait_send()

        @pl.when(has_low)
        def _():
            halo_low(g).wait_send()
            start_low(g).wait_send()

    @pl.loop(0, slabs)
    def _(other):
        remote(
            turned.at[:, pl.ds(0, rows)],
            columns.at[:, :, pl.ds(pl.multiple_of(other * local, local), local)],
            turn_send.at[other],
            turn_recv.at[other],
            partner,
            other,
        ).wait_recv()

    @pl.loop(0, slabs)
    def _(other):
        turn(other).wait_send()


def smooth(slabs, columns, matrix, source_out, decay_out):
    slab = lax.axis_index("slab")
    _, rows, _, nx = columns.shape
    width = source_out.shape[2]
    for kind, out in enumerate((source_out, decay_out)):
        for row in range(rows):
            result = jnp.dot(
                matrix[...], columns[kind, row], precision=lax.Precision.HIGHEST, preferred_element_type=jnp.float32
            )
            if width < nx:
                out[0] = pltpu.roll(result, lax.rem(nx - lax.rem(slab * width, nx), nx), axis=1)[:, :width]
            else:
                out[0, :, pl.ds(row * nx, nx)] = result


def solution(mesh):
    groups, slabs = mesh.shape["tm"], mesh.shape["slab"]
    placed = (
        P("tm", None, "slab", None, None),
        P("tm", "slab", None, None),
        P("slab", None, None),
        P("tm", None, "slab", None, None),
        P(),
        P(),
    )

    def body(initial, source, decay_rate, observed, release, smooth_taps):
        _, channels, local, ny, nx = initial.shape
        depth = local * slabs
        width = ny * nx // slabs
        rows = max(1, width // nx)
        assert groups % 2 == 0 and local >= WIDE
        assert width % nx == 0 or nx % width == 0
        f32 = jnp.float32
        anywhere = pl.BlockSpec(memory_space=pl.ANY)
        out = jax.ShapeDtypeStruct((1, depth, width), f32)
        dma = pltpu.SemaphoreType.DMA
        columns, matrix = pl.pallas_call(
            functools.partial(kernel, groups, slabs),
            out_shape=(
                jax.ShapeDtypeStruct((2, rows, depth, nx), f32),
                jax.ShapeDtypeStruct((depth, depth), f32),
            ),
            in_specs=[anywhere] * 6,
            out_specs=[anywhere, pl.BlockSpec(memory_space=pltpu.VMEM)],
            scratch_shapes=[
                pltpu.VMEM((channels, local + 2 * WIDE, ny, nx), f32),
                pltpu.VMEM((local + 2 * SIDE, ny, nx), f32),
                pltpu.VMEM((local + 2 * SIDE, ny, nx), f32),
                pltpu.VMEM((channels, STEPS - 1, local, ny, nx), f32),
                pltpu.VMEM((channels, local, ny, nx), f32),
                pltpu.VMEM((channels, local + 2 * SIDE, ny, nx), f32),
                pltpu.VMEM((2, local, ny, nx), f32),
                pltpu.VMEM((2, ny, local, nx), f32),
                pltpu.SMEM(release.shape, jnp.int32),
                pltpu.SMEM(smooth_taps.shape, f32),
                dma((5,)),
                dma((4,)),
                dma((4,)),
                dma((2, channels // GROUP)),
                dma((2, channels // GROUP)),
                dma((channels // GROUP,)),
                dma((channels // GROUP,)),
                dma((2, channels // GROUP)),
                dma((2, channels // GROUP)),
                dma((slabs,)),
                dma((slabs,)),
            ],
            compiler_params=pltpu.CompilerParams(
                collective_id=0, has_side_effects=True, vmem_limit_bytes=60 * 1024 * 1024
            ),
        )(release, smooth_taps, initial, source, decay_rate, observed)
        vmem = pl.BlockSpec(memory_space=pltpu.VMEM)
        return pl.pallas_call(
            functools.partial(smooth, slabs), out_shape=(out, out), in_specs=[vmem, vmem], out_specs=[vmem, vmem]
        )(columns, matrix)

    return jax.shard_map(
        body,
        mesh=mesh,
        in_specs=placed,
        out_specs=(P("tm", None, "slab"), P("tm", None, "slab")),
        check_vma=False,
    )
```

```python
import functools

import jax
import jax.numpy as jnp
from jax import lax
from jax.experimental import pallas as pl
from jax.experimental.pallas import tpu as pltpu
from jax.sharding import PartitionSpec as P

STEPS = 4
LANES = 128
vertical_rate = 0.2
lateral_rate = 0.1

MESH = pl.DeviceIdType.MESH
WIDE = STEPS
GROUP = 2
LAG = 1
SIDE = STEPS - 1


def operator(v, centre, edges):
    left, right, front, back = edges
    middle = v[1:-1]
    count, ny, nx = middle.shape
    flat = middle.reshape(count * ny, nx)
    west = pltpu.roll(flat, 1, axis=1).reshape(middle.shape)
    east = pltpu.roll(flat, nx - 1, axis=1).reshape(middle.shape)
    south = pltpu.roll(flat, 1, axis=0).reshape(middle.shape)
    north = pltpu.roll(flat, count * ny - 1, axis=0).reshape(middle.shape)
    lateral = west * left + east * right + south * front + north * back
    return middle * centre + vertical_rate * (v[2:] + v[:-2]) + lateral


def inside(v, width, low, high):
    return jnp.concatenate([v[:width] * low, v[width:-width], v[-width:] * high], axis=0)


def kernel(
    groups,
    slabs,
    release_in,
    taps_in,
    initial_ref,
    source_ref,
    decay_ref,
    observed_ref,
    columns,
    matrix,
    start,
    centre,
    field,
    states,
    target,
    adjoint,
    total,
    turned,
    release_ref,
    taps_ref,
    local_sem,
    side_send,
    side_recv,
    start_send,
    start_recv,
    obs_send,
    obs_recv,
    halo_send,
    halo_recv,
    turn_send,
    turn_recv,
):
    tm = lax.axis_index("tm")
    slab = lax.axis_index("slab")
    partner = lax.rem(tm + groups // 2, groups)
    channels, _, ny, nx = start.shape
    local = decay_ref.shape[0]
    parcels = channels // GROUP
    depth = matrix.shape[0]
    rows = columns.shape[1]
    width = ny * nx // slabs
    has_low = slab > 0
    has_high = slab < slabs - 1

    def local_copies():
        return (
            pltpu.make_async_copy(initial_ref.at[0], start.at[:, pl.ds(WIDE, local)], local_sem.at[0]),
            pltpu.make_async_copy(source_ref.at[0], field.at[pl.ds(SIDE, local)], local_sem.at[1]),
            pltpu.make_async_copy(decay_ref, centre.at[pl.ds(SIDE, local)], local_sem.at[2]),
            pltpu.make_async_copy(release_in, release_ref, local_sem.at[3]),
            pltpu.make_async_copy(taps_in, taps_ref, local_sem.at[4]),
        )

    def remote(src, dst, send, recv, to_tm, to_slab):
        return pltpu.make_async_remote_copy(
            src_ref=src,
            dst_ref=dst,
            send_sem=send,
            recv_sem=recv,
            device_id=(to_tm, to_slab),
            device_id_type=MESH,
        )

    def to_high():
        other = slab + 1
        return (
            remote(decay_ref.at[pl.ds(local - SIDE, SIDE)], centre.at[pl.ds(0, SIDE)], side_send.at[0], side_recv.at[0], tm, other),
            remote(source_ref.at[0, pl.ds(local - SIDE, SIDE)], field.at[pl.ds(0, SIDE)], side_send.at[1], side_recv.at[1], tm, other),
        )

    def to_low():
        other = slab - 1
        return (
            remote(decay_ref.at[pl.ds(0, SIDE)], centre.at[pl.ds(SIDE + local, SIDE)], side_send.at[2], side_recv.at[2], tm, other),
            remote(source_ref.at[0, pl.ds(0, SIDE)], field.at[pl.ds(SIDE + local, SIDE)], side_send.at[3], side_recv.at[3], tm, other),
        )

    def span(g):
        return pl.ds(g * GROUP, GROUP)

    def start_high(g):
        return remote(
            initial_ref.at[0, span(g), pl.ds(local - WIDE, WIDE)], start.at[span(g), pl.ds(0, WIDE)], start_send.at[0, g], start_recv.at[0, g], tm, slab + 1
        )

    def start_low(g):
        return remote(
            initial_ref.at[0, span(g), pl.ds(0, WIDE)], start.at[span(g), pl.ds(WIDE + local, WIDE)], start_send.at[1, g], start_recv.at[1, g], tm, slab - 1
        )

    def observation(g):
        return remote(observed_ref.at[0, span(g)], target.at[span(g)], obs_send.at[g], obs_recv.at[g], partner, slab)

    def halo_high(g):
        return remote(
            adjoint.at[span(g), pl.ds(local, SIDE)], adjoint.at[span(g), pl.ds(0, SIDE)], halo_send.at[0, g], halo_recv.at[0, g], tm, slab + 1
        )

    def halo_low(g):
        return remote(
            adjoint.at[span(g), pl.ds(SIDE, SIDE)], adjoint.at[span(g), pl.ds(SIDE + local, SIDE)], halo_send.at[1, g], halo_recv.at[1, g], tm, slab - 1
        )

    def turn(other):
        return remote(
            turned.at[:, pl.ds((other * width) // nx, rows)],
            columns.at[:, :, pl.ds(pl.multiple_of(slab * local, local), local)],
            turn_send.at[other],
            turn_recv.at[slab],
            partner,
            other,
        )

    for copy in local_copies():
        copy.start()

    barrier = pltpu.get_barrier_semaphore()

    @pl.loop(0, slabs)
    def _(other):
        pl.semaphore_signal(barrier, inc=1, device_id=(partner, other), device_id_type=MESH)

    @pl.when(has_low)
    def _():
        pl.semaphore_signal(barrier, inc=1, device_id=(tm, slab - 1), device_id_type=MESH)

    @pl.when(has_high)
    def _():
        pl.semaphore_signal(barrier, inc=1, device_id=(tm, slab + 1), device_id_type=MESH)

    pl.semaphore_wait(barrier, slabs + has_low.astype(jnp.int32) + has_high.astype(jnp.int32))

    observation(0).start()

    @pl.when(has_high)
    def _():
        for copy in to_high():
            copy.start()

    @pl.when(has_low)
    def _():
        for copy in to_low():
            copy.start()

    @pl.loop(0, parcels)
    def _(g):
        @pl.when(has_high)
        def _():
            start_high(g).start()

        @pl.when(has_low)
        def _():
            start_low(g).start()

        @pl.when(g > 0)
        def _():
            observation(g).start()

    @pl.when(jnp.logical_not(has_low))
    def _():
        centre[pl.ds(0, SIDE)] = jnp.zeros((SIDE, ny, nx), jnp.float32)
        field[pl.ds(0, SIDE)] = jnp.zeros((SIDE, ny, nx), jnp.float32)
        start[:, pl.ds(0, WIDE)] = jnp.zeros((channels, WIDE, ny, nx), jnp.float32)
        adjoint[:, pl.ds(0, SIDE)] = jnp.zeros((channels, SIDE, ny, nx), jnp.float32)

    @pl.when(jnp.logical_not(has_high))
    def _():
        centre[pl.ds(SIDE + local, SIDE)] = jnp.zeros((SIDE, ny, nx), jnp.float32)
        field[pl.ds(SIDE + local, SIDE)] = jnp.zeros((SIDE, ny, nx), jnp.float32)
        start[:, pl.ds(WIDE + local, WIDE)] = jnp.zeros((channels, WIDE, ny, nx), jnp.float32)
        adjoint[:, pl.ds(SIDE + local, SIDE)] = jnp.zeros((channels, SIDE, ny, nx), jnp.float32)

    low = jnp.where(has_low, 1.0, 0.0).astype(jnp.float32)
    high = jnp.where(has_high, 1.0, 0.0).astype(jnp.float32)

    for copy in local_copies():
        copy.wait()

    taps = taps_ref.shape[0]
    offset = (
        lax.broadcasted_iota(jnp.int32, (depth, depth), 1)
        - lax.broadcasted_iota(jnp.int32, (depth, depth), 0)
        + (taps - 1) // 2
    )
    matrix[...] = jnp.zeros_like(matrix)
    for tap in range(taps):
        matrix[...] += jnp.where(offset == tap, taps_ref[tap], 0.0)

    total[...] = jnp.zeros_like(total)

    x_at = lax.broadcasted_iota(jnp.int32, (ny, nx), 1)
    y_at = lax.broadcasted_iota(jnp.int32, (ny, nx), 0)
    edges = tuple(
        jnp.where(place, 0.0, lateral_rate).astype(jnp.float32)
        for place in (x_at == 0, x_at == nx - 1, y_at == 0, y_at == ny - 1)
    )

    @pl.when(has_low)
    def _():
        for copy in to_high():
            copy.wait_recv()

    @pl.when(has_high)
    def _():
        for copy in to_low():
            copy.wait_recv()

    centre[...] = (1.0 - 2.0 * vertical_rate - 4.0 * lateral_rate) - centre[...]

    def forward(c):
        when = release_ref[tm, c]
        current = start[c]
        for step in range(STEPS):
            halo = SIDE - step
            chosen = jnp.where(when == step, 1.0, 0.0).astype(jnp.float32)
            part = pl.ds(step, local + 2 * halo)
            current = operator(current, centre[part], edges) + chosen * field[part]
            if halo:
                current = inside(current, halo, low, high)
                states[c, step] = current[halo:-halo]
            else:
                adjoint[c, pl.ds(SIDE, local)] = current

    def backward(c):
        when = release_ref[tm, c]
        current = adjoint[c]
        decay_sum = total[1]
        source_sum = total[0]
        for step in reversed(range(STEPS)):
            own = current[step : step + local]
            chosen = jnp.where(when == step, 1.0, 0.0).astype(jnp.float32)
            source_sum = source_sum + chosen * own
            past = states[c, step - 1] if step else start[c, pl.ds(WIDE, local)]
            decay_sum = decay_sum - own * past
            if step:
                halo = step - 1
                current = operator(current, centre[pl.ds(SIDE - halo, local + 2 * halo)], edges)
                if halo:
                    current = inside(current, halo, low, high)
        total[0] = source_sum
        total[1] = decay_sum

    def members(g, action):
        for c in range(GROUP):
            action(g * GROUP + c)

    def settle(g):
        @pl.when(has_low)
        def _():
            halo_high(g).wait_recv()

        @pl.when(has_high)
        def _():
            halo_low(g).wait_recv()

        members(g, backward)

    @pl.loop(0, parcels)
    def _(g):
        @pl.when(has_low)
        def _():
            start_high(g).wait_recv()

        @pl.when(has_high)
        def _():
            start_low(g).wait_recv()

        members(g, forward)
        observation(g).wait_recv()
        adjoint[span(g), pl.ds(SIDE, local)] = adjoint[span(g), pl.ds(SIDE, local)] - target[span(g)]

        @pl.when(has_high)
        def _():
            halo_high(g).start()

        @pl.when(has_low)
        def _():
            halo_low(g).start()

        @pl.when(g >= LAG)
        def _():
            settle(g - LAG)

    @pl.loop(parcels - LAG, parcels)
    def _(g):
        settle(g)

    for kind in range(2):
        turned[kind] = jnp.swapaxes(total[kind], 0, 1)

    @pl.loop(0, slabs)
    def _(step):
        turn(lax.rem(slab + slabs // 2 + step, slabs)).start()

    @pl.when(has_high)
    def _():
        for copy in to_high():
            copy.wait_send()

    @pl.when(has_low)
    def _():
        for copy in to_low():
            copy.wait_send()

    @pl.loop(0, parcels)
    def _(g):
        observation(g).wait_send()

        @pl.when(has_high)
        def _():
            halo_high(g).wait_send()
            start_high(g).wait_send()

        @pl.when(has_low)
        def _():
            halo_low(g).wait_send()
            start_low(g).wait_send()

    @pl.loop(0, slabs)
    def _(other):
        remote(
            turned.at[:, pl.ds(0, rows)],
            columns.at[:, :, pl.ds(pl.multiple_of(other * local, local), local)],
            turn_send.at[other],
            turn_recv.at[other],
            partner,
            other,
        ).wait_recv()

    @pl.loop(0, slabs)
    def _(other):
        turn(other).wait_send()


def smooth(slabs, columns, matrix, source_out, decay_out):
    slab = lax.axis_index("slab")
    _, rows, _, nx = columns.shape
    width = source_out.shape[2]
    pieces = [columns[kind, row] for kind in range(2) for row in range(rows)]
    result = jnp.dot(
        matrix[...],
        jnp.concatenate(pieces, axis=1),
        precision=lax.Precision.HIGHEST,
        preferred_element_type=jnp.float32,
    )
    for kind, out in enumerate((source_out, decay_out)):
        part = result[:, kind * rows * nx : (kind + 1) * rows * nx]
        if width < nx:
            part = pltpu.roll(part, lax.rem(nx - lax.rem(slab * width, nx), nx), axis=1)[:, :width]
        out[0] = part


def solution(mesh):
    groups, slabs = mesh.shape["tm"], mesh.shape["slab"]
    placed = (
        P("tm", None, "slab", None, None),
        P("tm", "slab", None, None),
        P("slab", None, None),
        P("tm", None, "slab", None, None),
        P(),
        P(),
    )

    def body(initial, source, decay_rate, observed, release, smooth_taps):
        _, channels, local, ny, nx = initial.shape
        depth = local * slabs
        width = ny * nx // slabs
        rows = max(1, width // nx)
        assert groups % 2 == 0 and local >= WIDE
        assert width % nx == 0 or nx % width == 0
        f32 = jnp.float32
        anywhere = pl.BlockSpec(memory_space=pl.ANY)
        out = jax.ShapeDtypeStruct((1, depth, width), f32)
        dma = pltpu.SemaphoreType.DMA
        columns, matrix = pl.pallas_call(
            functools.partial(kernel, groups, slabs),
            out_shape=(
                jax.ShapeDtypeStruct((2, rows, depth, nx), f32),
                jax.ShapeDtypeStruct((depth, depth), f32),
            ),
            in_specs=[anywhere] * 6,
            out_specs=[anywhere, pl.BlockSpec(memory_space=pltpu.VMEM)],
            scratch_shapes=[
                pltpu.VMEM((channels, local + 2 * WIDE, ny, nx), f32),
                pltpu.VMEM((local + 2 * SIDE, ny, nx), f32),
                pltpu.VMEM((local + 2 * SIDE, ny, nx), f32),
                pltpu.VMEM((channels, STEPS - 1, local, ny, nx), f32),
                pltpu.VMEM((channels, local, ny, nx), f32),
                pltpu.VMEM((channels, local + 2 * SIDE, ny, nx), f32),
                pltpu.VMEM((2, local, ny, nx), f32),
                pltpu.VMEM((2, ny, local, nx), f32),
                pltpu.SMEM(release.shape, jnp.int32),
                pltpu.SMEM(smooth_taps.shape, f32),
                dma((5,)),
                dma((4,)),
                dma((4,)),
                dma((2, channels // GROUP)),
                dma((2, channels // GROUP)),
                dma((channels // GROUP,)),
                dma((channels // GROUP,)),
                dma((2, channels // GROUP)),
                dma((2, channels // GROUP)),
                dma((slabs,)),
                dma((slabs,)),
            ],
            compiler_params=pltpu.CompilerParams(
                collective_id=0, has_side_effects=True, vmem_limit_bytes=60 * 1024 * 1024
            ),
        )(release, smooth_taps, initial, source, decay_rate, observed)
        vmem = pl.BlockSpec(memory_space=pltpu.VMEM)
        return pl.pallas_call(
            functools.partial(smooth, slabs), out_shape=(out, out), in_specs=[vmem, vmem], out_specs=[vmem, vmem]
        )(columns, matrix)

    return jax.shard_map(
        body,
        mesh=mesh,
        in_specs=placed,
        out_specs=(P("tm", None, "slab"), P("tm", None, "slab")),
        check_vma=False,
    )
```
